32 devices in a mesh: row: 4 (over z), col: 4 (over y, x), rep: 2 (over core).
Axes of the slice: x: 2, y: 2, z: 4, core: 2. Of those that a mesh axis runs over, the one named last changes fastest.
Arguments:
- tokens: bfloat16 [128, 4096], P(('col', 'rep'), 'row'), may hold values from -6 to 6
- grad_out: bfloat16 [128, 4096], P(('col', 'rep'), 'row'), may hold values from -2.5 to 2.5
- gate_weight: bfloat16 [4096, 14336], P('row', 'col'), may hold values from -0.09375 to 0.09375
- up_weight: bfloat16 [4096, 14336], P('row', 'col'), may hold values from -0.09375 to 0.09375
- down_weight: bfloat16 [14336, 4096], P('col', 'row'), may hold values from -0.046875 to 0.046875
- gate_keep: int32 [32, 112], P('row', 'col'), may hold values from 0 to 1, as said below
- up_keep: int32 [32, 112], P('row', 'col'), may hold values from 0 to 1, as said below
- down_keep: int32 [112, 32], P('col', 'row'), may hold values from 0 to 1, as said below
Outputs:
- mixed: bfloat16 [128, 4096], P(('col', 'rep'), 'row')
- input_grad: bfloat16 [128, 4096], P(('col', 'rep'), 'row')
- gate_weight_grad: bfloat16 [4096, 14336], P('row', 'col')
- up_weight_grad: bfloat16 [4096, 14336], P('row', 'col')
- down_weight_grad: bfloat16 [14336, 4096], P('col', 'row')
The draws below stay inside these ranges and needn't reach their ends.
Inputs may be any that keep to these rules, and one draw needn't show every extreme that they name: `gate_keep`: 1 keeps the 128 x 128 block of the gate projection, 0 prunes it; the kept share differs from one device's region to the next. `up_keep`: 1 keeps the 128 x 128 block of the up projection, 0 prunes it; the kept share differs from one device's region to the next. `down_keep`: 1 keeps the 128 x 128 block of the down projection, 0 prunes it; the kept share differs from one device's region to the next.
All inputs are finite; a program needn't handle non-finite values.
Results may differ from the reference program's by a relative error of at most 0.025.
Values may be sent and summed in bfloat16 or wider, within the bound.
A program may use at most 128 MiB of HBM per device.

```python
import jax
import jax.numpy as jnp
from jax import lax

D = 4096
FF = 14336
BLOCK = 128
TOK_DEV = 16
TOKENS = 128
ROW_BLOCKS = 8
COL_BLOCKS = 28
N_ROW = 4
N_COL = 4
N_REP = 2


def keep_pattern(key, block_rows, block_cols, group_rows, group_cols):
    level_key, cell_key = jax.random.split(key)
    levels = jax.random.randint(level_key, (block_rows // group_rows, block_cols // group_cols), 1, 9)
    cells = jax.random.randint(cell_key, (block_rows, block_cols), 0, 8)
    spread = jnp.repeat(jnp.repeat(levels, group_rows, axis=0), group_cols, axis=1)
    return (cells < spread).astype(jnp.int32)


def draw_gate_keep(key, part):
    return keep_pattern(jax.random.fold_in(key, 11), D // BLOCK, FF // BLOCK, ROW_BLOCKS, COL_BLOCKS)


def draw_up_keep(key, part):
    return keep_pattern(jax.random.fold_in(key, 23), D // BLOCK, FF // BLOCK, ROW_BLOCKS, COL_BLOCKS)


def draw_down_keep(key, part):
    return keep_pattern(jax.random.fold_in(key, 37), FF // BLOCK, D // BLOCK, COL_BLOCKS, ROW_BLOCKS)


def block_scale(own_key, shape, pieces, low, high):
    gain, own = 1.0, jax.random.fold_in(own_key, 6)
    for dim, blocks in pieces:
        draws = jnp.exp(jax.random.uniform(jax.random.fold_in(own, dim), (blocks,), jnp.float32, low / len(pieces), high / len(pieces)))
        gain = gain * jnp.repeat(draws, shape[dim] // blocks).reshape([-1 if axis == dim else 1 for axis in range(len(shape))])
    return gain


def scatter_about(stream_key, extent, scale, most, cuts=(), kind=jnp.bfloat16):
    level = block_scale(stream_key, extent, cuts, -0.22, 0.18) if cuts else 1.0
    array = jax.random.normal(stream_key, extent, jnp.float32) * scale * level
    return jnp.minimum(jnp.maximum(array, -most), most).astype(kind)


def setup_inputs(seed: int = 0) -> dict:
    key_list = jax.random.split(jax.random.key(seed), 9)
    tokens = scatter_about(key_list[0], (TOKENS, D), 1.0, 6.0, ((0, 8), (1, 4)))
    grad_out = scatter_about(key_list[1], (TOKENS, D), 0.25, 2.5, ((0, 8), (1, 4)))
    gate_weight = scatter_about(key_list[2], (D, FF), D ** -0.5, 0.09375, ((0, 4), (1, 4)))
    up_weight = scatter_about(key_list[3], (D, FF), D ** -0.5, 0.09375, ((0, 4), (1, 4)))
    down_weight = scatter_about(key_list[4], (FF, D), FF ** -0.5, 0.046875, ((0, 4), (1, 4)))
    gate_keep = draw_gate_keep(jax.random.fold_in(key_list[8], 71), 0)
    up_keep = draw_up_keep(jax.random.fold_in(key_list[8], 71), 0)
    down_keep = draw_down_keep(jax.random.fold_in(key_list[8], 71), 0)
    return {"tokens": tokens, "grad_out": grad_out, "gate_weight": gate_weight, "up_weight": up_weight, "down_weight": down_weight, "gate_keep": gate_keep, "up_keep": up_keep, "down_keep": down_keep}


def masked(weight, keep):
    rows, cols = keep.shape
    tiled = weight.reshape(rows, weight.shape[0] // rows, cols, weight.shape[1] // cols)
    return (tiled * keep[:, None, :, None].astype(weight.dtype)).reshape(weight.shape)


def rounded(value):
    narrow = lax.optimization_barrier(value.astype(jnp.bfloat16))
    return narrow.astype(jnp.float32)


def block_sum(left, weight):
    size = left.shape[1] // N_ROW

    def step(total, index):
        begin = (index * size).astype(jnp.int32)
        part_left = lax.dynamic_slice_in_dim(left, begin, size, 1)
        part_weight = lax.dynamic_slice_in_dim(weight, begin, size, 0)
        partial_value = jnp.dot(part_left, part_weight, preferred_element_type=jnp.float32)
        return total + rounded(partial_value), None

    start_total = jnp.zeros((left.shape[0], weight.shape[1]), jnp.float32)
    total, unused = lax.scan(step, start_total, jnp.arange(N_ROW, dtype=jnp.int32))
    return total


def reference(tokens, grad_out, gate_weight, up_weight, down_weight, gate_keep, up_keep, down_keep):
    gate_eff = masked(gate_weight, gate_keep)
    up_eff = masked(up_weight, up_keep)
    down_eff = masked(down_weight, down_keep)
    token_groups = tokens.reshape(N_COL, N_REP, TOK_DEV, D)
    grad_groups = grad_out.reshape(N_COL, N_REP, TOK_DEV, D)
    mixed_list = []
    input_list = []
    gate_total = jnp.zeros((D, FF), jnp.float32)
    up_total = jnp.zeros((D, FF), jnp.float32)
    down_total = jnp.zeros((FF, D), jnp.float32)
    for replica in range(N_REP):
        x_rows = token_groups[:, replica].reshape(N_COL * TOK_DEV, D)
        dy_rows = grad_groups[:, replica].reshape(N_COL * TOK_DEV, D)
        gate_sum = block_sum(x_rows, gate_eff)
        up_sum = block_sum(x_rows, up_eff)
        gate_sig = jax.nn.sigmoid(gate_sum)
        hidden = (gate_sum * gate_sig * up_sum).astype(jnp.bfloat16)
        mixed = jnp.dot(hidden, down_eff, preferred_element_type=jnp.float32).astype(jnp.bfloat16)
        back_sum = block_sum(dy_rows, down_eff.T)
        gate_grad = (back_sum * up_sum * gate_sig * (1.0 + gate_sum * (1.0 - gate_sig))).astype(jnp.bfloat16)
        up_grad = (back_sum * gate_sum * gate_sig).astype(jnp.bfloat16)
        input_grad = jnp.dot(gate_grad, gate_eff.T, preferred_element_type=jnp.float32)
        input_grad = (input_grad + jnp.dot(up_grad, up_eff.T, preferred_element_type=jnp.float32)).astype(jnp.bfloat16)
        gate_term = masked(jnp.dot(x_rows.T, gate_grad, preferred_element_type=jnp.float32), gate_keep)
        up_term = masked(jnp.dot(x_rows.T, up_grad, preferred_element_type=jnp.float32), up_keep)
        down_term = masked(jnp.dot(hidden.T, dy_rows, preferred_element_type=jnp.float32), down_keep)
        gate_total = gate_total + rounded(gate_term)
        up_total = up_total + rounded(up_term)
        down_total = down_total + rounded(down_term)
        mixed_list.append(mixed.reshape(N_COL, TOK_DEV, D))
        input_list.append(input_grad.reshape(N_COL, TOK_DEV, D))
    mixed_all = jnp.stack(mixed_list, axis=1).reshape(TOKENS, D)
    input_all = jnp.stack(input_list, axis=1).reshape(TOKENS, D)
    return (mixed_all, input_all, gate_total.astype(jnp.bfloat16), up_total.astype(jnp.bfloat16), down_total.astype(jnp.bfloat16))
```

```python
import functools

import jax
import jax.numpy as jnp
from jax import lax
from jax.experimental import pallas as pl
from jax.experimental.pallas import tpu as pltpu
from jax.sharding import PartitionSpec as P

PLAIN = (((1,), (0,)), ((), ()))
FLIPPED = (((1,), (1,)), ((), ()))
OVER_ROWS = (((0,), (0,)), ((), ()))
MESH = pl.DeviceIdType.MESH
BLOCK = 128
F32 = jnp.float32
BF16 = jnp.bfloat16


def masked(weight, keep):
    rows, cols = keep.shape
    tiled = weight.reshape(rows, weight.shape[0] // rows, cols, weight.shape[1] // cols)
    return (tiled * keep[:, None, :, None].astype(weight.dtype)).reshape(weight.shape)


def product(left, weight, flipped):
    return lax.dot_general(
        left, weight, FLIPPED if flipped else PLAIN, preferred_element_type=F32
    )


def swiglu_grads(back, gate_value, gate_sig, up_value):
    gate_grad = (back * up_value * gate_sig * (1.0 + gate_value * (1.0 - gate_sig))).astype(BF16)
    up_grad = (back * gate_value * gate_sig).astype(BF16)
    return (gate_grad, up_grad)


def plain_device(
    tokens, grad_out, gate_weight, up_weight, down_weight, gate_keep, up_keep, down_keep
):
    model_block = tokens.shape[1]
    gate_used = masked(gate_weight, gate_keep)
    up_used = masked(up_weight, up_keep)
    down_used = masked(down_weight, down_keep)
    token_panel = lax.all_gather(tokens, "col", axis=0, tiled=True)
    grad_panel = lax.all_gather(grad_out, "col", axis=0, tiled=True)
    gate_part = product(token_panel, gate_used, False)
    up_part = product(token_panel, up_used, False)
    back_part = product(grad_panel, down_used, True)
    gate_sum, up_sum, back_sum = (
        lax.psum(part.astype(BF16), "row").astype(F32) for part in (gate_part, up_part, back_part)
    )
    gate_sig = jax.nn.sigmoid(gate_sum)
    hidden = (gate_sum * gate_sig * up_sum).astype(BF16)
    gate_grad, up_grad = swiglu_grads(back_sum, gate_sum, gate_sig, up_sum)
    both = lambda value: lax.all_gather(value, "rep", axis=0, tiled=True)
    tokens_all, grads_all, hidden_all, gate_all, up_all = (
        both(value) for value in (token_panel, grad_panel, hidden, gate_grad, up_grad)
    )
    over = lambda left, right, keep: masked(
        lax.dot_general(left, right, OVER_ROWS, preferred_element_type=F32), keep
    ).astype(BF16)
    forward = product(hidden, down_used, False)
    backward = product(gate_grad, gate_used, True) + product(up_grad, up_used, True)
    combined = lax.psum_scatter(
        jnp.concatenate([forward, backward], axis=1).astype(BF16),
        "col",
        scatter_dimension=0,
        tiled=True,
    )
    return (
        combined[:, :model_block],
        combined[:, model_block:],
        over(tokens_all, gate_all, gate_keep),
        over(tokens_all, up_all, up_keep),
        over(hidden_all, grads_all, down_keep),
    )


def layer_kernel(
    n, n_col,
    x_ref, dy_ref, gate_ref, up_ref, down_ref, gk_ref, uk_ref, dk_ref,
    mixed_ref, input_ref, xp_ref, yp_ref, h_ref,
    w, d, part, sums, arrived, acc_m, acc_i, parts_out, parts_in,
    load_sem, ag_send, ag_recv, hop_send, hop_recv, bc_send, bc_recv, pt_send, pt_recv,
    rs_send, rs_recv,
):
    me, c, r = lax.axis_index("row"), lax.axis_index("col"), lax.axis_index("rep")
    peers = 2 * n_col
    index = c * 2 + r
    rows = x_ref.shape[0]
    nb = w.shape[0]
    half = nb // 2
    model_blocks = x_ref.shape[1] // BLOCK

    def loads(b):
        g = r * nb + b
        cols = pl.ds(pl.multiple_of(g * BLOCK, BLOCK), BLOCK)
        return (
            pltpu.make_async_copy(gate_ref.at[:, cols], w.at[b, :, pl.ds(0, BLOCK)], load_sem.at[0, b]),
            pltpu.make_async_copy(up_ref.at[:, cols], w.at[b, :, pl.ds(BLOCK, BLOCK)], load_sem.at[1, b]),
            pltpu.make_async_copy(down_ref.at[cols], d.at[b], load_sem.at[2, b]),
        )

    def start_loads(j, carry):
        for base in (0, half):
            for copy in loads(base + j):
                copy.start()
        return carry

    barrier = pltpu.get_barrier_semaphore()
    others = [lax.rem(index + o, peers) for o in range(1, peers)]
    for other in others:
        pl.semaphore_signal(barrier, inc=1, device_id=(me, other // 2, other % 2), device_id_type=MESH)

    @pl.when(me > 0)
    def _():
        pl.semaphore_signal(barrier, inc=1, device_id=(me - 1, c, r), device_id_type=MESH)

    @pl.when(me < n - 1)
    def _():
        pl.semaphore_signal(barrier, inc=1, device_id=(me + 1, c, r), device_id_type=MESH)

    lax.fori_loop(0, half, start_loads, 0)
    edges = jnp.where(me > 0, 1, 0) + jnp.where(me < n - 1, 1, 0)
    pl.semaphore_wait(barrier, peers - 1 + edges)

    def panel(src, dst, kind, owner, target):
        return pltpu.make_async_remote_copy(
            src_ref=src,
            dst_ref=dst.at[pl.ds(pl.multiple_of(owner * rows, rows), rows)],
            send_sem=ag_send.at[kind, target],
            recv_sem=ag_recv.at[kind, owner],
            device_id=(me, target // 2, target % 2),
            device_id_type=MESH,
        )

    for other in others:
        panel(x_ref, xp_ref, 0, index, other).start()
        panel(dy_ref, yp_ref, 1, index, other).start()
    own = pl.ds(pl.multiple_of(index * rows, rows), rows)
    xp_ref[own] = x_ref[...]
    yp_ref[own] = dy_ref[...]
    acc_m[...] = jnp.zeros_like(acc_m)
    acc_i[...] = jnp.zeros_like(acc_i)
    for other in others:
        panel(x_ref, xp_ref, 0, other, other).wait_recv()
        panel(dy_ref, yp_ref, 1, other, other).wait_recv()

    def compute(b):
        for copy in loads(b):
            copy.wait()
        g = r * nb + b
        for a in range(model_blocks):
            span = pl.ds(a * BLOCK, BLOCK)
            first, second = pl.ds(0, BLOCK), pl.ds(BLOCK, BLOCK)
            w[b, span, first] = (w[b, span, first].astype(F32) * gk_ref[a, g].astype(F32)).astype(BF16)
            w[b, span, second] = (w[b, span, second].astype(F32) * uk_ref[a, g].astype(F32)).astype(BF16)
            d[b, :, span] = (d[b, :, span].astype(F32) * dk_ref[g, a].astype(F32)).astype(BF16)
        part[b, :, pl.ds(0, 2 * BLOCK)] = product(xp_ref[...], w[b], False)
        part[b, :, pl.ds(2 * BLOCK, BLOCK)] = product(yp_ref[...], d[b], True)

    def hop_copy(b, device):
        return pltpu.make_async_remote_copy(
            src_ref=sums.at[b],
            dst_ref=arrived.at[b],
            send_sem=hop_send.at[b],
            recv_sem=hop_recv.at[b],
            device_id=(device, c, r),
            device_id_type=MESH,
        )

    def cast_copy(b, device):
        g = r * nb + b
        return pltpu.make_async_remote_copy(
            src_ref=h_ref.at[g],
            dst_ref=h_ref.at[g],
            send_sem=bc_send.at[b],
            recv_sem=bc_recv.at[b],
            device_id=(device, c, r),
            device_id_type=MESH,
        )

    def pair_copy(b, rep):
        g = rep * nb + b
        return pltpu.make_async_remote_copy(
            src_ref=h_ref.at[g],
            dst_ref=h_ref.at[g],
            send_sem=pt_send.at[b],
            recv_sem=pt_recv.at[b],
            device_id=(me, c, 1 - r),
            device_id_type=MESH,
        )

    def hop(j, pos, before, after, base):
        @pl.when((j >= 0) & (j < half))
        def _():
            b = base + j

            @pl.when(pos > 0)
            def _():
                hop_copy(b, before).wait_recv()
                part[b] = part[b] + arrived[b].astype(F32)

            @pl.when(pos < n - 1)
            def _():
                sums[b] = part[b].astype(BF16)
                hop_copy(b, after).start()

            @pl.when(pos == n - 1)
            def _():
                gate_sum = part[b, :, pl.ds(0, BLOCK)]
                up_sum = part[b, :, pl.ds(BLOCK, BLOCK)]
                back_sum = part[b, :, pl.ds(2 * BLOCK, BLOCK)]
                gate_sig = jax.nn.sigmoid(gate_sum)
                gate_grad, up_grad = swiglu_grads(back_sum, gate_sum, gate_sig, up_sum)
                g = r * nb + b
                h_ref[g, :, pl.ds(0, BLOCK)] = (gate_sum * gate_sig * up_sum).astype(BF16)
                h_ref[g, :, pl.ds(BLOCK, BLOCK)] = gate_grad
                h_ref[g, :, pl.ds(2 * BLOCK, BLOCK)] = up_grad

    def cast(j, pos, before, after, base):
        @pl.when((j >= 0) & (j < half))
        def _():
            b = base + j

            @pl.when(pos < n - 1)
            def _():
                cast_copy(b, after).wait_recv()

            @pl.when(pos > 0)
            def _():
                cast_copy(b, before).start()

            pair_copy(b, r).start()

    def consume(j, base):
        @pl.when((j >= 0) & (j < half))
        def _():
            b = base + j
            g = r * nb + b
            acc_m[...] += product(h_ref[g, :, pl.ds(0, BLOCK)], d[b], False)
            acc_i[...] += product(h_ref[g, :, pl.ds(BLOCK, 2 * BLOCK)], w[b], True)

    back = n - 1 - me
    low, high = me - 1, me + 1
    ways = ((me, low, high, 0), (back, high, low, half))

    compute(0)
    compute(half)

    def step(t, carry):
        for pos, before, after, base in ways:
            hop(t - pos, pos, before, after, base)
        for pos, before, after, base in ways:
            cast(t - 2 * (n - 1) + pos, pos, before, after, base)

        @pl.when(t + 1 < half)
        def _():
            compute(t + 1)
            compute(half + t + 1)

        for pos, before, after, base in ways:
            consume(t - 2 * (n - 1) + pos, base)
        return carry

    lax.fori_loop(0, half + 2 * (n - 1), step, 0)

    for p in range(peers):
        span = pl.ds(p * rows, rows)
        parts_out[p, pl.ds(0, rows)] = acc_m[span].astype(BF16)
        parts_out[p, pl.ds(rows, rows)] = acc_i[span].astype(BF16)

    def share(owner, source):
        return pltpu.make_async_remote_copy(
            src_ref=parts_out.at[owner],
            dst_ref=parts_in.at[source],
            send_sem=rs_send.at[owner],
            recv_sem=rs_recv.at[source],
            device_id=(me, owner // 2, owner % 2),
            device_id_type=MESH,
        )

    for other in others:
        share(other, index).start()
    total = parts_out[index].astype(F32)

    def drain(b, carry):
        pair_copy(b, r).wait_send()
        pair_copy(b, 1 - r).wait_recv()
        return carry

    lax.fori_loop(0, nb, drain, 0)
    for pos, before, after, base in ways:

        @pl.when(pos < n - 1)
        def _():
            def body(j, carry):
                hop_copy(base + j, after).wait_send()
                return carry

            lax.fori_loop(0, half, body, 0)

        @pl.when(pos > 0)
        def _():
            def body(j, carry):
                cast_copy(base + j, before).wait_send()
                return carry

            lax.fori_loop(0, half, body, 0)

    for other in others:
        panel(x_ref, xp_ref, 0, index, other).wait_send()
        panel(dy_ref, yp_ref, 1, index, other).wait_send()
    for other in others:
        pltpu.make_async_remote_copy(
            src_ref=parts_out.at[other],
            dst_ref=parts_in.at[other],
            send_sem=rs_send.at[other],
            recv_sem=rs_recv.at[other],
            device_id=(me, other // 2, other % 2),
            device_id_type=MESH,
        ).wait_recv()
        total = total + parts_in[other].astype(F32)
    mixed_ref[...] = total[:rows].astype(BF16)
    input_ref[...] = total[rows:].astype(BF16)
    for other in others:
        share(other, index).wait_send()


def weight_kernel(x_ref, y_ref, h_ref, gk_ref, uk_ref, dk_ref, gate_ref, up_ref, down_ref, xt):
    s = pl.program_id(0)
    wide = h_ref.shape[0]
    model_blocks = x_ref.shape[1] // BLOCK

    @pl.when(s == 0)
    def _():
        xt[...] = x_ref[...].T

    for i in range(wide):
        g = s * wide + i
        cols = pl.ds(i * BLOCK, BLOCK)
        grads = h_ref[i, :, pl.ds(BLOCK, 2 * BLOCK)]
        hidden = h_ref[i, :, pl.ds(0, BLOCK)].T
        for a in range(model_blocks):
            span = pl.ds(a * BLOCK, BLOCK)
            term = product(xt[span], grads, False)
            gate_ref[span, cols] = (term[:, :BLOCK] * gk_ref[a, g].astype(F32)).astype(BF16)
            up_ref[span, cols] = (term[:, BLOCK:] * uk_ref[a, g].astype(F32)).astype(BF16)
            down = product(hidden, y_ref[:, span], False)
            down_ref[cols, span] = (down * dk_ref[g, a].astype(F32)).astype(BF16)


def kernel_device(
    n, n_col,
    tokens, grad_out, gate_weight, up_weight, down_weight, gate_keep, up_keep, down_keep,
):
    rows, model = tokens.shape
    hidden = gate_weight.shape[1]
    everyone = 2 * n_col * rows
    peers = 2 * n_col
    nb = hidden // (2 * BLOCK)
    vmem = pl.BlockSpec(memory_space=pltpu.VMEM)
    smem = pl.BlockSpec(memory_space=pltpu.SMEM)
    far = pl.BlockSpec(memory_space=pl.ANY)
    dma = pltpu.SemaphoreType.DMA
    mixed, input_grad, token_panel, grad_panel, hidden_blocks = pl.pallas_call(
        functools.partial(layer_kernel, n, n_col),
        out_shape=(
            jax.ShapeDtypeStruct((rows, model), BF16),
            jax.ShapeDtypeStruct((rows, model), BF16),
            jax.ShapeDtypeStruct((everyone, model), BF16),
            jax.ShapeDtypeStruct((everyone, model), BF16),
            jax.ShapeDtypeStruct((2 * nb, everyone, 3 * BLOCK), BF16),
        ),
        in_specs=[vmem, vmem, far, far, far, smem, smem, smem],
        out_specs=(vmem,) * 5,
        scratch_shapes=[
            pltpu.VMEM((nb, model, 2 * BLOCK), BF16),
            pltpu.VMEM((nb, BLOCK, model), BF16),
            pltpu.VMEM((nb, everyone, 3 * BLOCK), F32),
            pltpu.VMEM((nb, everyone, 3 * BLOCK), BF16),
            pltpu.VMEM((nb, everyone, 3 * BLOCK), BF16),
            pltpu.VMEM((everyone, model), F32),
            pltpu.VMEM((everyone, model), F32),
            pltpu.VMEM((peers, 2 * rows, model), BF16),
            pltpu.VMEM((peers, 2 * rows, model), BF16),
            dma((3, nb)),
            dma((2, peers)),
            dma((2, peers)),
            dma((nb,)),
            dma((nb,)),
            dma((nb,)),
            dma((nb,)),
            dma((nb,)),
            dma((nb,)),
            dma((peers,)),
            dma((peers,)),
        ],
        compiler_params=pltpu.CompilerParams(
            collective_id=0, has_side_effects=True, vmem_limit_bytes=56 * 1024 * 1024
        ),
        name="layer",
    )(tokens, grad_out, gate_weight, up_weight, down_weight, gate_keep, up_keep, down_keep)
    wide = 2
    whole = pl.BlockSpec((everyone, model), lambda s: (0, 0))
    gate_grad, up_grad, down_grad = pl.pallas_call(
        weight_kernel,
        grid=(2 * nb // wide,),
        out_shape=(
            jax.ShapeDtypeStruct((model, hidden), BF16),
            jax.ShapeDtypeStruct((model, hidden), BF16),
            jax.ShapeDtypeStruct((hidden, model), BF16),
        ),
        in_specs=[
            whole,
            whole,
            pl.BlockSpec((wide, everyone, 3 * BLOCK), lambda s: (s, 0, 0)),
            smem,
            smem,
            smem,
        ],
        out_specs=(
            pl.BlockSpec((model, wide * BLOCK), lambda s: (0, s)),
            pl.BlockSpec((model, wide * BLOCK), lambda s: (0, s)),
            pl.BlockSpec((wide * BLOCK, model), lambda s: (s, 0)),
        ),
        scratch_shapes=[pltpu.VMEM((model, everyone), BF16)],
        compiler_params=pltpu.CompilerParams(vmem_limit_bytes=32 * 1024 * 1024),
        name="weights",
    )(token_panel, grad_panel, hidden_blocks, gate_keep, up_keep, down_keep)
    return mixed, input_grad, gate_grad, up_grad, down_grad


def per_device(n, n_col, n_rep, *args):
    tokens, gate_weight = args[0], args[2]
    rows, model = tokens.shape
    hidden = gate_weight.shape[1]
    fits = (
        n_rep == 2
        and n > 1
        and rows % 16 == 0
        and (2 * n_col * rows) % 128 == 0
        and model % 128 == 0
        and hidden % (4 * BLOCK) == 0
    )
    if fits:
        return kernel_device(n, n_col, *args)
    return plain_device(*args)


def solution(mesh):
    shape = mesh.shape
    return jax.shard_map(
        functools.partial(per_device, shape["row"], shape["col"], shape["rep"]),
        mesh=mesh,
        in_specs=(
            P(("col", "rep"), "row"),
            P(("col", "rep"), "row"),
            P("row", "col"),
            P("row", "col"),
            P("col", "row"),
            P("row", "col"),
            P("row", "col"),
            P("col", "row"),
        ),
        out_specs=(
            P(("col", "rep"), "row"),
            P(("col", "rep"), "row"),
            P("row", "col"),
            P("row", "col"),
            P("col", "row"),
        ),
        check_vma=False,
    )
```

```python
import functools

import jax
import jax.numpy as jnp
from jax import lax
from jax.experimental import pallas as pl
from jax.experimental.pallas import tpu as pltpu
from jax.sharding import PartitionSpec as P

PLAIN = (((1,), (0,)), ((), ()))
FLIPPED = (((1,), (1,)), ((), ()))
OVER_ROWS = (((0,), (0,)), ((), ()))
MESH = pl.DeviceIdType.MESH
BLOCK = 128
SPLIT = 2
LAG = 2
F32 = jnp.float32
BF16 = jnp.bfloat16


def masked(weight, keep):
    rows, cols = keep.shape
    tiled = weight.reshape(rows, weight.shape[0] // rows, cols, weight.shape[1] // cols)
    return (tiled * keep[:, None, :, None].astype(weight.dtype)).reshape(weight.shape)


def product(left, weight, flipped):
    return lax.dot_general(
        left, weight, FLIPPED if flipped else PLAIN, preferred_element_type=F32
    )


def swiglu_grads(back, gate_value, gate_sig, up_value):
    gate_grad = (back * up_value * gate_sig * (1.0 + gate_value * (1.0 - gate_sig))).astype(BF16)
    up_grad = (back * gate_value * gate_sig).astype(BF16)
    return (gate_grad, up_grad)


def plain_device(
    tokens, grad_out, gate_weight, up_weight, down_weight, gate_keep, up_keep, down_keep
):
    model_block = tokens.shape[1]
    gate_used = masked(gate_weight, gate_keep)
    up_used = masked(up_weight, up_keep)
    down_used = masked(down_weight, down_keep)
    token_panel = lax.all_gather(tokens, "col", axis=0, tiled=True)
    grad_panel = lax.all_gather(grad_out, "col", axis=0, tiled=True)
    gate_part = product(token_panel, gate_used, False)
    up_part = product(token_panel, up_used, False)
    back_part = product(grad_panel, down_used, True)
    gate_sum, up_sum, back_sum = (
        lax.psum(part.astype(BF16), "row").astype(F32) for part in (gate_part, up_part, back_part)
    )
    gate_sig = jax.nn.sigmoid(gate_sum)
    hidden = (gate_sum * gate_sig * up_sum).astype(BF16)
    gate_grad, up_grad = swiglu_grads(back_sum, gate_sum, gate_sig, up_sum)
    both = lambda value: lax.all_gather(value, "rep", axis=0, tiled=True)
    tokens_all, grads_all, hidden_all, gate_all, up_all = (
        both(value) for value in (token_panel, grad_panel, hidden, gate_grad, up_grad)
    )
    over = lambda left, right, keep: masked(
        lax.dot_general(left, right, OVER_ROWS, preferred_element_type=F32), keep
    ).astype(BF16)
    forward = product(hidden, down_used, False)
    backward = product(gate_grad, gate_used, True) + product(up_grad, up_used, True)
    combined = lax.psum_scatter(
        jnp.concatenate([forward, backward], axis=1).astype(BF16),
        "col",
        scatter_dimension=0,
        tiled=True,
    )
    return (
        combined[:, :model_block],
        combined[:, model_block:],
        over(tokens_all, gate_all, gate_keep),
        over(tokens_all, up_all, up_keep),
        over(hidden_all, grads_all, down_keep),
    )


def layer_kernel(
    n, n_col,
    x_ref, dy_ref, gate_ref, up_ref, down_ref, gk_ref, uk_ref, dk_ref,
    mixed_ref, input_ref, xp_ref, yp_ref, h_ref,
    w, d, part, sums, arrived, acc_m, acc_i, parts_out, parts_in,
    load_sem, ag_send, ag_recv, hop_send, hop_recv, bc_send, bc_recv, pt_send, pt_recv,
    rs_send, rs_recv,
):
    me, c, r = lax.axis_index("row"), lax.axis_index("col"), lax.axis_index("rep")
    peers = 2 * n_col
    index = c * 2 + r
    chunk = xp_ref.shape[0] // SPLIT
    rows = x_ref.shape[0]
    nb = w.shape[0]
    half = nb // 2
    model_blocks = x_ref.shape[1] // BLOCK

    def loads(b):
        g = r * nb + b
        cols = pl.ds(pl.multiple_of(g * BLOCK, BLOCK), BLOCK)
        return (
            pltpu.make_async_copy(gate_ref.at[:, cols], w.at[b, :, pl.ds(0, BLOCK)], load_sem.at[0, b]),
            pltpu.make_async_copy(up_ref.at[:, cols], w.at[b, :, pl.ds(BLOCK, BLOCK)], load_sem.at[1, b]),
            pltpu.make_async_copy(down_ref.at[cols], d.at[b], load_sem.at[2, b]),
        )

    def start_loads(j, carry):
        for base in (0, half):
            for copy in loads(base + j):
                copy.start()
        return carry

    barrier = pltpu.get_barrier_semaphore()
    others = [lax.rem(index + o, peers) for o in range(1, peers)]
    for other in others:
        pl.semaphore_signal(barrier, inc=1, device_id=(me, other // 2, other % 2), device_id_type=MESH)

    @pl.when(me > 0)
    def _():
        pl.semaphore_signal(barrier, inc=1, device_id=(me - 1, c, r), device_id_type=MESH)

    @pl.when(me < n - 1)
    def _():
        pl.semaphore_signal(barrier, inc=1, device_id=(me + 1, c, r), device_id_type=MESH)

    lax.fori_loop(0, half, start_loads, 0)
    edges = jnp.where(me > 0, 1, 0) + jnp.where(me < n - 1, 1, 0)
    pl.semaphore_wait(barrier, peers - 1 + edges)

    def panel(src, dst, kind, owner, target):
        return pltpu.make_async_remote_copy(
            src_ref=src,
            dst_ref=dst.at[pl.ds(pl.multiple_of(owner * rows, rows), rows)],
            send_sem=ag_send.at[kind, target],
            recv_sem=ag_recv.at[kind, owner],
            device_id=(me, target // 2, target % 2),
            device_id_type=MESH,
        )

    for other in others:
        panel(x_ref, xp_ref, 0, index, other).start()
        panel(dy_ref, yp_ref, 1, index, other).start()
    own = pl.ds(pl.multiple_of(index * rows, rows), rows)
    xp_ref[own] = x_ref[...]
    yp_ref[own] = dy_ref[...]
    acc_m[...] = jnp.zeros_like(acc_m)
    acc_i[...] = jnp.zeros_like(acc_i)
    for other in others:
        panel(x_ref, xp_ref, 0, other, other).wait_recv()
        panel(dy_ref, yp_ref, 1, other, other).wait_recv()

    def compute(b):
        for copy in loads(b):
            copy.wait()
        g = r * nb + b
        for a in range(model_blocks):
            span = pl.ds(a * BLOCK, BLOCK)
            first, second = pl.ds(0, BLOCK), pl.ds(BLOCK, BLOCK)
            w[b, span, first] = (w[b, span, first].astype(F32) * gk_ref[a, g].astype(F32)).astype(BF16)
            w[b, span, second] = (w[b, span, second].astype(F32) * uk_ref[a, g].astype(F32)).astype(BF16)
            d[b, :, span] = (d[b, :, span].astype(F32) * dk_ref[a, g].astype(F32)).astype(BF16)
        part[b, :, pl.ds(0, 2 * BLOCK)] = product(xp_ref[...], w[b], False)
        part[b, :, pl.ds(2 * BLOCK, BLOCK)] = product(yp_ref[...], d[b], True)

    def place(q):
        return q // SPLIT, pl.ds(pl.multiple_of(lax.rem(q, SPLIT) * chunk, chunk), chunk)

    def hop_copy(q, device):
        b, span = place(q)
        return pltpu.make_async_remote_copy(
            src_ref=sums.at[b, span],
            dst_ref=arrived.at[b, span],
            send_sem=hop_send.at[q],
            recv_sem=hop_recv.at[q],
            device_id=(device, c, r),
            device_id_type=MESH,
        )

    def cast_copy(q, device):
        b, span = place(q)
        g = r * nb + b
        return pltpu.make_async_remote_copy(
            src_ref=h_ref.at[g, span],
            dst_ref=h_ref.at[g, span],
            send_sem=bc_send.at[q],
            recv_sem=bc_recv.at[q],
            device_id=(device, c, r),
            device_id_type=MESH,
        )

    def pair_copy(q, rep):
        b, span = place(q)
        g = rep * nb + b
        return pltpu.make_async_remote_copy(
            src_ref=h_ref.at[g, span],
            dst_ref=h_ref.at[g, span],
            send_sem=pt_send.at[q],
            recv_sem=pt_recv.at[q],
            device_id=(me, c, 1 - r),
            device_id_type=MESH,
        )

    def hop(j, pos, before, after, base):
        @pl.when((j >= 0) & (j < count))
        def _():
            q = base + j
            b, span = place(q)

            @pl.when(pos > 0)
            def _():
                hop_copy(q, before).wait_recv()
                part[b, span] = part[b, span] + arrived[b, span].astype(F32)

            @pl.when(pos < n - 1)
            def _():
                sums[b, span] = part[b, span].astype(BF16)
                hop_copy(q, after).start()

            @pl.when(pos == n - 1)
            def _():
                gate_sum = part[b, span, pl.ds(0, BLOCK)]
                up_sum = part[b, span, pl.ds(BLOCK, BLOCK)]
                back_sum = part[b, span, pl.ds(2 * BLOCK, BLOCK)]
                gate_sig = jax.nn.sigmoid(gate_sum)
                gate_grad, up_grad = swiglu_grads(back_sum, gate_sum, gate_sig, up_sum)
                g = r * nb + b
                h_ref[g, span, pl.ds(0, BLOCK)] = (gate_sum * gate_sig * up_sum).astype(BF16)
                h_ref[g, span, pl.ds(BLOCK, BLOCK)] = gate_grad
                h_ref[g, span, pl.ds(2 * BLOCK, BLOCK)] = up_grad

    def cast(j, pos, before, after, base):
        @pl.when((j >= 0) & (j < count))
        def _():
            q = base + j
            b, span = place(q)

            @pl.when(pos < n - 1)
            def _():
                cast_copy(q, after).wait_recv()

            @pl.when(pos > 0)
            def _():
                cast_copy(q, before).start()

            pair_copy(q, r).start()

    def consume(j, base):
        @pl.when((j >= 0) & (j < count))
        def _():
            q = base + j
            b, span = place(q)
            g = r * nb + b
            acc_m[span] += product(h_ref[g, span, pl.ds(0, BLOCK)], d[b], False)
            acc_i[span] += product(h_ref[g, span, pl.ds(BLOCK, 2 * BLOCK)], w[b], True)

    back = n - 1 - me
    low, high = me - 1, me + 1
    count = half * SPLIT
    ways = ((me, low, high, 0), (back, high, low, count))

    compute(0)
    compute(half)

    def step(t, carry):
        for pos, before, after, base in ways:
            hop(t - LAG * pos, pos, before, after, base)
        for pos, before, after, base in ways:
            cast(t - LAG * (2 * (n - 1) - pos), pos, before, after, base)

        @pl.when((lax.rem(t + 1, SPLIT) == 0) & (t + 1 < count))
        def _():
            compute((t + 1) // SPLIT)
            compute(half + (t + 1) // SPLIT)

        for pos, before, after, base in ways:
            consume(t - LAG * (2 * (n - 1) - pos), base)
        return carry

    lax.fori_loop(0, count + LAG * 2 * (n - 1), step, 0)

    for p in range(peers):
        span = pl.ds(p * rows, rows)
        parts_out[p, pl.ds(0, rows)] = acc_m[span].astype(BF16)
        parts_out[p, pl.ds(rows, rows)] = acc_i[span].astype(BF16)

    def share(owner, source):
        return pltpu.make_async_remote_copy(
            src_ref=parts_out.at[owner],
            dst_ref=parts_in.at[source],
            send_sem=rs_send.at[owner],
            recv_sem=rs_recv.at[source],
            device_id=(me, owner // 2, owner % 2),
            device_id_type=MESH,
        )

    for other in others:
        share(other, index).start()
    total = parts_out[index].astype(F32)

    def drain(b, carry):
        pair_copy(b, r).wait_send()
        pair_copy(b, 1 - r).wait_recv()
        return carry

    lax.fori_loop(0, nb * SPLIT, drain, 0)
    for pos, before, after, base in ways:

        @pl.when(pos < n - 1)
        def _():
            def body(j, carry):
                hop_copy(base + j, after).wait_send()
                return carry

            lax.fori_loop(0, count, body, 0)

        @pl.when(pos > 0)
        def _():
            def body(j, carry):
                cast_copy(base + j, before).wait_send()
                return carry

            lax.fori_loop(0, count, body, 0)

    for other in others:
        panel(x_ref, xp_ref, 0, index, other).wait_send()
        panel(dy_ref, yp_ref, 1, index, other).wait_send()
    for other in others:
        pltpu.make_async_remote_copy(
            src_ref=parts_out.at[other],
            dst_ref=parts_in.at[other],
            send_sem=rs_send.at[other],
            recv_sem=rs_recv.at[other],
            device_id=(me, other // 2, other % 2),
            device_id_type=MESH,
        ).wait_recv()
        total = total + parts_in[other].astype(F32)
    mixed_ref[...] = total[:rows].astype(BF16)
    input_ref[...] = total[rows:].astype(BF16)
    for other in others:
        share(other, index).wait_send()


def weight_kernel(
    x_ref, y_ref, h_ref, m_ref, i_ref, gk_ref, uk_ref, dk_ref,
    gate_ref, up_ref, down_ref, mixed_ref, input_ref, xt,
):
    s = pl.program_id(0)
    wide = h_ref.shape[0]
    model = x_ref.shape[1]
    tall = 2 * BLOCK if model % (2 * BLOCK) == 0 else BLOCK

    @pl.when(s == 0)
    def _():
        xt[...] = x_ref[...].T
        mixed_ref[...] = m_ref[...]
        input_ref[...] = i_ref[...]

    for i in range(wide):
        g = s * wide + i
        cols = pl.ds(i * BLOCK, BLOCK)
        grads = h_ref[i, :, pl.ds(BLOCK, 2 * BLOCK)]
        hidden = h_ref[i, :, pl.ds(0, BLOCK)].T
        for begin in range(0, model, tall):
            term = product(xt[pl.ds(begin, tall)], grads, False)
            down = product(hidden, y_ref[:, pl.ds(begin, tall)], False)
            for inner in range(0, tall, BLOCK):
                a = (begin + inner) // BLOCK
                span = pl.ds(begin + inner, BLOCK)
                part = term[inner : inner + BLOCK]
                gate_ref[span, cols] = (part[:, :BLOCK] * gk_ref[a, g].astype(F32)).astype(BF16)
                up_ref[span, cols] = (part[:, BLOCK:] * uk_ref[a, g].astype(F32)).astype(BF16)
                down_ref[cols, span] = (
                    down[:, inner : inner + BLOCK] * dk_ref[a, g].astype(F32)
                ).astype(BF16)


def kernel_device(
    n, n_col,
    tokens, grad_out, gate_weight, up_weight, down_weight, gate_keep, up_keep, down_keep,
):
    rows, model = tokens.shape
    down_keep = down_keep.T
    hidden = gate_weight.shape[1]
    everyone = 2 * n_col * rows
    peers = 2 * n_col
    nb = hidden // (2 * BLOCK)
    vmem = pl.BlockSpec(memory_space=pltpu.VMEM)
    smem = pl.BlockSpec(memory_space=pltpu.SMEM)
    far = pl.BlockSpec(memory_space=pl.ANY)
    dma = pltpu.SemaphoreType.DMA
    mixed, input_grad, token_panel, grad_panel, hidden_blocks = pl.pallas_call(
        functools.partial(layer_kernel, n, n_col),
        out_shape=(
            jax.ShapeDtypeStruct((rows, model), BF16),
            jax.ShapeDtypeStruct((rows, model), BF16),
            jax.ShapeDtypeStruct((everyone, model), BF16),
            jax.ShapeDtypeStruct((everyone, model), BF16),
            jax.ShapeDtypeStruct((2 * nb, everyone, 3 * BLOCK), BF16),
        ),
        in_specs=[vmem, vmem, far, far, far, smem, smem, smem],
        out_specs=(vmem,) * 5,
        scratch_shapes=[
            pltpu.VMEM((nb, model, 2 * BLOCK), BF16),
            pltpu.VMEM((nb, BLOCK, model), BF16),
            pltpu.VMEM((nb, everyone, 3 * BLOCK), F32),
            pltpu.VMEM((nb, everyone, 3 * BLOCK), BF16),
            pltpu.VMEM((nb, everyone, 3 * BLOCK), BF16),
            pltpu.VMEM((everyone, model), F32),
            pltpu.VMEM((everyone, model), F32),
            pltpu.VMEM((peers, 2 * rows, model), BF16),
            pltpu.VMEM((peers, 2 * rows, model), BF16),
            dma((3, nb)),
            dma((2, peers)),
            dma((2, peers)),
            dma((nb * SPLIT,)),
            dma((nb * SPLIT,)),
            dma((nb * SPLIT,)),
            dma((nb * SPLIT,)),
            dma((nb * SPLIT,)),
            dma((nb * SPLIT,)),
            dma((peers,)),
            dma((peers,)),
        ],
        compiler_params=pltpu.CompilerParams(
            collective_id=0, has_side_effects=True, vmem_limit_bytes=56 * 1024 * 1024
        ),
        name="layer",
    )(tokens, grad_out, gate_weight, up_weight, down_weight, gate_keep, up_keep, down_keep)
    wide = 2
    whole = pl.BlockSpec((everyone, model), lambda s: (0, 0))
    small = pl.BlockSpec((rows, model), lambda s: (0, 0))
    gate_grad, up_grad, down_grad, mixed, input_grad = pl.pallas_call(
        weight_kernel,
        grid=(2 * nb // wide,),
        out_shape=(
            jax.ShapeDtypeStruct((model, hidden), BF16),
            jax.ShapeDtypeStruct((model, hidden), BF16),
            jax.ShapeDtypeStruct((hidden, model), BF16),
            jax.ShapeDtypeStruct((rows, model), BF16),
            jax.ShapeDtypeStruct((rows, model), BF16),
        ),
        in_specs=[
            whole,
            whole,
            pl.BlockSpec((wide, everyone, 3 * BLOCK), lambda s: (s, 0, 0)),
            small,
            small,
            smem,
            smem,
            smem,
        ],
        out_specs=(
            pl.BlockSpec((model, wide * BLOCK), lambda s: (0, s)),
            pl.BlockSpec((model, wide * BLOCK), lambda s: (0, s)),
            pl.BlockSpec((wide * BLOCK, model), lambda s: (s, 0)),
            small,
            small,
        ),
        scratch_shapes=[pltpu.VMEM((model, everyone), BF16)],
        compiler_params=pltpu.CompilerParams(vmem_limit_bytes=60 * 1024 * 1024),
        name="weights",
    )(token_panel, grad_panel, hidden_blocks, mixed, input_grad, gate_keep, up_keep, down_keep)
    return mixed, input_grad, gate_grad, up_grad, down_grad


def per_device(n, n_col, n_rep, *args):
    tokens, gate_weight = args[0], args[2]
    rows, model = tokens.shape
    hidden = gate_weight.shape[1]
    fits = (
        n_rep == 2
        and n > 1
        and rows % 16 == 0
        and (2 * n_col * rows) % (64 * SPLIT) == 0
        and model % 128 == 0
        and hidden % (4 * BLOCK) == 0
    )
    if fits:
        return kernel_device(n, n_col, *args)
    return plain_device(*args)


def solution(mesh):
    shape = mesh.shape
    return jax.shard_map(
        functools.partial(per_device, shape["row"], shape["col"], shape["rep"]),
        mesh=mesh,
        in_specs=(
            P(("col", "rep"), "row"),
            P(("col", "rep"), "row"),
            P("row", "col"),
            P("row", "col"),
            P("col", "row"),
            P("row", "col"),
            P("row", "col"),
            P("col", "row"),
        ),
        out_specs=(
            P(("col", "rep"), "row"),
            P(("col", "rep"), "row"),
            P("row", "col"),
            P("row", "col"),
            P("col", "row"),
        ),
        check_vma=False,
    )
```
